32 devices in a mesh: dp: 8 (over y, x, core), tensor: 4 (over z).
Axes of the slice: x: 2, y: 2, z: 4, core: 2. Of those that a mesh axis runs over, the one named last changes fastest.
Arguments:
- hidden_in: bfloat16 [2, 4096, 2048], P(None, ('dp', 'tensor')), may hold values from -6 to 6
- out_cotangent: bfloat16 [2, 4096, 2048], P(None, ('dp', 'tensor')), may hold values from -6 to 6
- piece_start: int32 [2, 8], P(None, 'dp'), may hold values from 0 to 256, as said below
- query_weight: bfloat16 [2048, 2048], P('dp', 'tensor'), may hold values from -0.1875 to 0.1875
- key_weight: bfloat16 [2048, 2048], P('dp', 'tensor'), may hold values from -0.1875 to 0.1875
- value_weight: bfloat16 [2048, 2048], P('dp', 'tensor'), may hold values from -0.125 to 0.125
- output_weight: bfloat16 [2048, 2048], P('tensor', 'dp'), may hold values from -0.75 to 0.75
- gate_weight: bfloat16 [2048, 8192], P('dp', 'tensor'), may hold values from -0.125 to 0.125
- up_weight: bfloat16 [2048, 8192], P('dp', 'tensor'), may hold values from -0.125 to 0.125
- down_weight: bfloat16 [8192, 2048], P('tensor', 'dp'), may hold values from -0.0625 to 0.0625
- attn_gain: bfloat16 [2048], P('dp'), may hold values from 0.25 to 1.75
- mlp_gain: bfloat16 [2048], P('dp'), may hold values from 0.25 to 1.75
- memory_gate: float32 [16], P('tensor'), may hold values from -2 to 2
Outputs:
- hidden_out: bfloat16 [2, 4096, 2048], P(None, ('dp', 'tensor'))
- hidden_grad: float32 [2, 4096, 2048], P(None, ('dp', 'tensor'))
- query_weight_grad: float32 [2048, 2048], P('dp', 'tensor')
- key_weight_grad: float32 [2048, 2048], P('dp', 'tensor')
- value_weight_grad: float32 [2048, 2048], P('dp', 'tensor')
- output_weight_grad: float32 [2048, 2048], P('tensor', 'dp')
- gate_weight_grad: float32 [2048, 8192], P('dp', 'tensor')
- up_weight_grad: float32 [2048, 8192], P('dp', 'tensor')
- down_weight_grad: float32 [8192, 2048], P('tensor', 'dp')
- attn_gain_grad: float32 [2048], P('dp')
- mlp_gain_grad: float32 [2048], P('dp')
- memory_gate_grad: float32 [16], P('tensor')
The draws below stay inside these ranges and needn't reach their ends.
Inputs may be any that keep to these rules, and one draw needn't show every extreme that they name: `piece_start`: each segment of 512 positions holds one picture piece of 256 positions, starting at this offset within the segment.
All inputs are finite; a program needn't handle non-finite values.
Results may differ from the reference program's by a relative error of at most 0.014.
The reference program's roundings to bfloat16 on the way count: a program that leaves them out, or rounds other values in their place, can miss the bound.
Values may be sent and summed in bfloat16 or wider, within the bound.
No kernel may reach another device: no remote copies, remote signals or barrier semaphores. Data moves between devices by JAX's collectives and lax.ppermute only.
A program may use at most 256 MiB of HBM per device.

```python
import jax
import jax.numpy as jnp
from jax import lax

D = 2048
HEADS = 16
HD = 128
FF = 8192
SEG = 512
PIECE = 256
MB = 2
SEGMENTS = 8


def draw_piece_start(key, part):
    starts = jax.random.randint(key, (MB, SEGMENTS), 0, SEG - PIECE + 1)
    starts = starts.at[0, 0].set(SEG - PIECE)
    starts = starts.at[MB - 1, SEGMENTS - 1].set(0)
    return starts.astype(jnp.int32)


def steps_of(key, dims, shards, smallest, largest):
    level, own = 1.0, jax.random.fold_in(key, 6)
    for position, parts in shards:
        steps = jnp.exp(jax.random.uniform(jax.random.fold_in(own, position), (parts,), jnp.float32, smallest / len(shards), largest / len(shards)))
        level = level * jnp.repeat(steps, dims[position] // parts).reshape([-1 if axis == position else 1 for axis in range(len(dims))])
    return level


def gaussian(key, dims, deviation, limit, pieces=(), held_as=jnp.bfloat16):
    gain = steps_of(key, dims, pieces, -0.22, 0.18) if pieces else 1.0
    array = jax.random.normal(key, dims, jnp.float32) * deviation * gain
    return jnp.minimum(jnp.maximum(array, -limit), limit).astype(held_as)


def setup_inputs(seed: int = 0) -> dict:
    keys = jax.random.split(jax.random.key(seed), 14)
    hidden_in = gaussian(keys[0], (MB, SEGMENTS * SEG, D), 1.0, 6.0, ((1, 32),))
    out_cotangent = gaussian(keys[1], (MB, SEGMENTS * SEG, D), 1.0, 6.0, ((1, 32),))
    piece_start = draw_piece_start(jax.random.fold_in(keys[13], 71), 0)
    query_weight = gaussian(keys[3], (D, HEADS * HD), (D // 2) ** -0.5, 0.1875, ((0, 8), (1, 4)))
    key_weight = gaussian(keys[4], (D, HEADS * HD), (D // 2) ** -0.5, 0.1875, ((0, 8), (1, 4)))
    value_weight = gaussian(keys[5], (D, HEADS * HD), D ** -0.5, 0.125, ((0, 8), (1, 4)))
    output_weight = gaussian(keys[6], (HEADS * HD, D), (D // 32) ** -0.5, 0.75, ((0, 4), (1, 8)))
    gate_weight = gaussian(keys[7], (D, FF), D ** -0.5, 0.125, ((0, 8), (1, 4)))
    up_weight = gaussian(keys[8], (D, FF), D ** -0.5, 0.125, ((0, 8), (1, 4)))
    down_weight = gaussian(keys[9], (FF, D), FF ** -0.5, 0.0625, ((0, 4), (1, 8)))
    attn_gain = jnp.clip(1.0 + 0.15 * jax.random.normal(keys[10], (D,), jnp.float32), 0.25, 1.75).astype(jnp.bfloat16)
    mlp_gain = jnp.clip(1.0 + 0.15 * jax.random.normal(keys[11], (D,), jnp.float32), 0.25, 1.75).astype(jnp.bfloat16)
    memory_gate = jnp.clip(jax.random.uniform(keys[12], (HEADS,), jnp.float32, -2.0, 2.0) * steps_of(keys[12], (HEADS,), ((0, 4),), -0.4, 0.0), -2.0, 2.0)
    return {"hidden_in": hidden_in, "out_cotangent": out_cotangent, "piece_start": piece_start, "query_weight": query_weight, "key_weight": key_weight, "value_weight": value_weight, "output_weight": output_weight, "gate_weight": gate_weight, "up_weight": up_weight, "down_weight": down_weight, "attn_gain": attn_gain, "mlp_gain": mlp_gain, "memory_gate": memory_gate}


@jax.custom_vjp
def low(v):
    return lax.optimization_barrier(v.astype(jnp.bfloat16)).astype(jnp.float32)

@jax.custom_vjp
def low_back(v):
    return v

def low_keep(v):
    return (low(v), None)

def low_pass(kept, grad):
    return (grad,)

def back_keep(v):
    return (v, None)

def back_low(kept, grad):
    return (low(grad),)
low.defvjp(low_keep, low_pass)
low_back.defvjp(back_keep, back_low)
epsilon = 1e-05
highest = lax.Precision.HIGHEST

def matmul_high(left_side, right_side):
    return jnp.dot(left_side, right_side, precision=highest)

def norm_rows(values, gain_row):
    return values * lax.rsqrt(lax.optimization_barrier(jnp.mean(values * values, axis=-1, keepdims=True)) + epsilon) * gain_row

def elu_plus(values):
    return jnp.where(values > 0, values, jnp.expm1(jnp.minimum(values, 0.0))) + 1.0

def segment_mix(state_in, segment_in, mixing):
    memory, normer = state_in
    queries, keys_in, values_in, offset = segment_in
    places = jnp.arange(SEG)
    inside = (places >= offset) & (places < offset + PIECE)
    allowed = (places[:, None] >= places[None, :]) | inside[:, None] & inside[None, :]
    scores = low_back(jnp.einsum('qhd,khd->hqk', queries, keys_in, precision=highest) * float(HD) ** (-0.5))
    scores = jnp.where(allowed[None], scores, -1e+30)
    score_peak = lax.optimization_barrier(jnp.max(scores, axis=-1, keepdims=True))
    exp_scores = jnp.exp(scores - score_peak)
    soft_probs = low(exp_scores / lax.optimization_barrier(jnp.sum(exp_scores, axis=-1, keepdims=True)))
    local_mix = low_back(jnp.einsum('hqk,khd->qhd', soft_probs, values_in, precision=highest))
    feature_q = elu_plus(queries)
    feature_k = elu_plus(keys_in)
    numerator = jnp.einsum('qhd,hde->qhe', feature_q, memory, precision=highest)
    denominator = jnp.einsum('qhd,hd->qh', feature_q, normer, precision=highest) + 1.0
    recalled = numerator / denominator[..., None]
    mixture = mixing[None, :, None] * recalled + (1.0 - mixing[None, :, None]) * local_mix
    memory = memory + jnp.einsum('khd,khe->hde', feature_k, values_in, precision=highest)
    normer = normer + lax.optimization_barrier(jnp.sum(feature_k, axis=0))
    return ((memory, normer), mixture)

def sequence_pass(params_in, tokens_in, offsets):
    query_full, key_full, value_full, output_full, gate_full, up_full, down_full, gain_one, gain_two, gate_logit = params_in
    normed = low(norm_rows(tokens_in, gain_one))

    def project(weight):
        return low(low_back(matmul_high(normed, weight))).reshape(SEGMENTS, SEG, HEADS, HD)
    queries = project(query_full)
    keys_all = project(key_full)
    values_all = project(value_full)
    mixing = jax.nn.sigmoid(gate_logit)

    def advance(state_in, segment_in):
        return segment_mix(state_in, segment_in, mixing)
    start_state = (jnp.zeros((HEADS, HD, HD), jnp.float32), jnp.zeros((HEADS, HD), jnp.float32))
    unused_state, mixture = lax.scan(advance, start_state, (queries, keys_all, values_all, offsets))
    heads_out = low(mixture.reshape(SEGMENTS * SEG, HEADS * HD))
    middle = tokens_in + low_back(matmul_high(heads_out, output_full))
    normed_two = low(norm_rows(middle, gain_two))
    gated = low_back(matmul_high(normed_two, gate_full))
    upper = low_back(matmul_high(normed_two, up_full))
    hidden_act = low(gated * jax.nn.sigmoid(gated) * upper)
    return middle + low_back(matmul_high(hidden_act, down_full))

def reference(hidden_in, out_cotangent, piece_start, query_weight, key_weight, value_weight, output_weight, gate_weight, up_weight, down_weight, attn_gain, mlp_gain, memory_gate):
    params = tuple((member.astype(jnp.float32) for member in (query_weight, key_weight, value_weight, output_weight, gate_weight, up_weight, down_weight, attn_gain, mlp_gain, memory_gate)))

    def forward(params_in, tokens_all):
        offsets = piece_start.astype(jnp.int32)

        def one_sequence(pair_in):
            return sequence_pass(params_in, pair_in[0], pair_in[1])
        return lax.map(jax.checkpoint(one_sequence), (tokens_all, offsets))
    hidden_out, pullback = jax.vjp(forward, params, hidden_in.astype(jnp.float32))
    gradients, hidden_grad = pullback(out_cotangent.astype(jnp.float32))
    return (hidden_out.astype(jnp.bfloat16), hidden_grad, gradients[0], gradients[1], gradients[2], gradients[3], gradients[4], gradients[5], gradients[6], gradients[7], gradients[8], gradients[9])
```

```python
import functools
from types import SimpleNamespace

import jax
import jax.numpy as jnp
from jax import lax
from jax.experimental import pallas as pl
from jax.experimental.pallas import tpu as pltpu
from jax.sharding import PartitionSpec as P

HD = 128
PIECE = 256
epsilon = 1e-05
highest = lax.Precision.HIGHEST
bf16 = jnp.bfloat16
f32 = jnp.float32


class Order:
    def __init__(self):
        self.last = None

    def place(self, values):
        if self.last is None:
            return values
        return lax.optimization_barrier((values, self.last))[0]

    def done(self, values):
        self.last = values
        return values


NEAR = [(0, 0), (0, 1), (2, 1), (2, 0), (6, 0), (6, 1), (4, 1), (4, 0)]


def far_bits(count):
    bits = [1]
    while 2 ** (2 + len(bits)) < count:
        bits.append(2 ** (2 + len(bits)))
    return bits


def half_order(count):
    order = list(NEAR)
    for bit in far_bits(count):
        order = order + [(offset | bit, half) for offset, half in order]
    return order


def flip(values, bit):
    count = lax.axis_size("dp")
    return lax.ppermute(values, "dp", [(i, i ^ bit) for i in range(count)])


def cut(values, parts, axis):
    size = values.shape[axis] // parts
    return [lax.slice_in_dim(values, k * size, (k + 1) * size, axis=axis) for k in range(parts)]


def join_kernel(axis, own_ref, a_ref, b_ref, far_0_ref, far_1_ref, out_ref):
    size = far_0_ref.shape[axis]

    def part(ref, place, count=1):
        where = slice(place * size, (place + count) * size)
        return (where, slice(None)) if axis == 0 else (slice(None), where)

    out_ref[part(out_ref, 0, 2)] = own_ref[...]
    out_ref[part(out_ref, 2)] = a_ref[part(a_ref, 1)]
    out_ref[part(out_ref, 3)] = a_ref[part(a_ref, 0)]
    out_ref[part(out_ref, 4)] = far_0_ref[...]
    out_ref[part(out_ref, 5)] = far_1_ref[...]
    out_ref[part(out_ref, 6)] = b_ref[part(b_ref, 1)]
    out_ref[part(out_ref, 7)] = b_ref[part(b_ref, 0)]


def join_blocks(own, near_a, near_b, far_0, far_1, axis):
    if axis == 1 and far_0.shape[1] % HD:
        a, b = cut(near_a, 2, axis), cut(near_b, 2, axis)
        return jnp.concatenate([own, a[1], a[0], far_0, far_1, b[1], b[0]], axis=axis)
    other = 1 - axis
    parts = 4 if own.shape[other] % (4 * HD) == 0 else 1
    shape = list(own.shape)
    shape[axis] *= 4

    def block(dims):
        dims = list(dims)
        dims[other] //= parts
        return pl.BlockSpec(tuple(dims), lambda j: (0, j) if axis == 0 else (j, 0))

    arrays = (own, near_a, near_b, far_0, far_1)
    return pl.pallas_call(
        functools.partial(join_kernel, axis),
        grid=(parts,),
        in_specs=[block(array.shape) for array in arrays],
        out_specs=block(shape),
        out_shape=jax.ShapeDtypeStruct(tuple(shape), own.dtype),
        compiler_params=params(),
        cost_estimate=cost(64, 64),
    )(*arrays)


class Spread:
    def __init__(self, order, own, axis):
        self.order, self.axis = order, axis
        self.own = order.place(own)
        self.near_a, self.near_b = flip(self.own, 2), flip(self.own, 4)

    def second(self):
        self.near_a, self.near_b = self.order.done(self.order.place((self.near_a, self.near_b)))
        b_0 = cut(self.near_b, 2, self.axis)[0]
        a_1 = cut(self.near_a, 2, self.axis)[1]
        self.far = flip(b_0, 2), flip(a_1, 4)

    def third(self):
        far = self.order.place(self.far)
        known = self.order.done(join_blocks(self.own, self.near_a, self.near_b, *far, self.axis))
        bits = far_bits(lax.axis_size("dp"))
        for bit in bits[:-1]:
            known = jnp.concatenate([known, flip(known, bit)], axis=self.axis)
        self.whole = known, flip(known, bits[-1])

    def arrive(self):
        self.whole = self.order.done(self.order.place(self.whole))


def plus(*terms):
    total = terms[0].astype(f32)
    for term in terms[1:]:
        total = total + term.astype(f32)
    return total


class Collect:
    def __init__(self, order, product, axis):
        self.order, self.product, self.axis = order, product, axis
        self.bits = far_bits(lax.axis_size("dp"))
        product_two = order.done(product(1))
        self.received = flip(product_two, self.bits[-1])

    def second(self):
        total = self.order.done(self.product(0, self.received))
        axis = self.axis
        for bit in reversed(self.bits[:-1]):
            one, two = cut(total, 2, axis)
            total = plus(one, flip(two, bit)).astype(bf16)
        self.parts = cut(total, 8, axis)
        size = self.parts[0].shape[axis]
        self.got_x = flip(lax.slice_in_dim(total, 3 * size, 5 * size, axis=axis), 2)
        self.got_y = flip(lax.slice_in_dim(total, 5 * size, 7 * size, axis=axis), 4)

    def third(self):
        got_x, got_y = self.order.place((self.got_x, self.got_y))
        self.mine_x, pass_x = cut(got_x, 2, self.axis)
        pass_y, self.mine_y = cut(got_y, 2, self.axis)
        go_x = plus(self.parts[2], pass_y).astype(bf16)
        go_y = plus(self.parts[7], pass_x).astype(bf16)
        go_x, go_y = self.order.done((go_x, go_y))
        self.last_x, self.last_y = flip(go_x, 2), flip(go_y, 4)

    def finish(self):
        self.last_x, self.last_y = self.order.place((self.last_x, self.last_y))
        return self.order.done(
            jnp.concatenate(
                [
                    plus(self.parts[0], self.mine_x, self.last_y),
                    plus(self.parts[1], self.last_x, self.mine_y),
                ],
                axis=self.axis,
            )
        )


def move_kernel(table_ref, *refs):
    count = len(refs) // 2
    pieces = table_ref.shape[0]
    width = refs[0].shape[-1] // pieces
    for source, target in zip(refs[:count], refs[count:]):
        for k in range(pieces):
            start = pl.multiple_of(table_ref[k] * width, width)
            target[..., k * width : (k + 1) * width] = source[..., pl.ds(start, width)]


def move_columns(arrays, table):
    width = arrays[0].shape[-1] // table.shape[0]
    if width % HD:
        return [
            jnp.concatenate(
                [
                    lax.dynamic_slice_in_dim(values, table[k] * width, width, axis=-1)
                    for k in range(table.shape[0])
                ],
                axis=-1,
            )
            for values in arrays
        ]
    vmem = pl.BlockSpec(memory_space=pltpu.VMEM)
    return pl.pallas_call(
        move_kernel,
        in_specs=[pl.BlockSpec(memory_space=pltpu.SMEM)] + [vmem for _ in arrays],
        out_specs=[vmem for _ in arrays],
        out_shape=[jax.ShapeDtypeStruct(values.shape, values.dtype) for values in arrays],
        compiler_params=pltpu.CompilerParams(vmem_limit_bytes=24 * 1024 * 1024),
    )(table, *arrays)


def tables(place, order):
    count = len(order) // 2
    inward = [[(own ^ offset) * 2 + half for offset, half in order] for own in range(count)]
    outward = [[row.index(block) for block in range(2 * count)] for row in inward]
    return [
        lax.dynamic_index_in_dim(jnp.asarray(table, jnp.int32), place, 0, False)
        for table in (inward, outward)
    ]


PAIRS = [(0, 1), (1, 0), (2, 3), (3, 2)]
MIDDLE = [(1, 2), (2, 1)]
OUTER = [(1, 0), (2, 3)]
INNER = [(0, 1), (3, 2)]


def send(values, pairs):
    return lax.ppermute(values, "tensor", pairs)


def at_end():
    place = lax.axis_index("tensor")
    return (place == 0) | (place == 3)


def slot_owner():
    place = lax.axis_index("tensor")
    low = place < 2
    return [place, place ^ 1, jnp.where(low, 2, 1), jnp.where(low, 3, 0)]


def offload_gather(own):
    return lax.all_gather(own, "tensor", axis=0, tiled=True)


class OffloadGather:
    def __init__(self, order, own):
        self.order = order
        self.whole = offload_gather(order.place(own))

    def finish(self):
        return self.whole


class OffloadScatter:
    def __init__(self, order, values):
        self.order = order
        self.own = lax.psum_scatter(values, "tensor", scatter_dimension=0, tiled=True)

    def finish(self):
        return self.order.place(self.own).astype(f32)


class Gather:
    def __init__(self, order, own):
        self.order = order
        self.own = order.place(own)
        self.partner = send(self.own, PAIRS)
        self.middle_near = send(self.own, MIDDLE)

    def second(self):
        self.partner, self.middle_near = self.order.done(
            self.order.place((self.partner, self.middle_near))
        )
        self.middle_far = send(self.partner, MIDDLE)
        self.outer_near = send(self.middle_near, OUTER)

    def third(self):
        self.middle_far, self.outer_near = self.order.done(
            self.order.place((self.middle_far, self.outer_near))
        )
        self.outer_far = send(self.middle_far, OUTER)

    def finish(self):
        outer_far = self.order.place(self.outer_far)
        end = at_end()
        near = jnp.where(end, self.outer_near, self.middle_near)
        far = jnp.where(end, outer_far, self.middle_far)
        rows = self.own.shape[0]
        whole = jnp.zeros((4 * rows, self.own.shape[1]), self.own.dtype)
        for owner, piece in zip(slot_owner(), (self.own, self.partner, near, far)):
            whole = lax.dynamic_update_slice_in_dim(whole, piece, owner * rows, axis=0)
        return self.order.done(whole)


class Scatter:
    def __init__(self, order, values):
        rows = values.shape[0] // 4
        self.order = order
        self.own, self.partner, self.near, self.far = [
            lax.dynamic_slice_in_dim(values, owner * rows, rows, axis=0) for owner in slot_owner()
        ]
        self.inner_far = send(self.far, INNER)
        self.inner_near = send(self.near, INNER)

    def second(self):
        go = self.order.done(plus(self.far, self.order.place(self.inner_far)).astype(bf16))
        self.middle_far = send(go, MIDDLE)

    def third(self):
        inner_near, middle_far = self.order.place((self.inner_near, self.middle_far))
        go_near = plus(self.near, inner_near).astype(bf16)
        go_pair = plus(self.partner, middle_far).astype(bf16)
        go_near, go_pair = self.order.done((go_near, go_pair))
        self.paired = send(go_pair, PAIRS)
        self.middle_near = send(go_near, MIDDLE)

    def finish(self):
        paired, middle_near = self.order.place((self.paired, self.middle_near))
        return plus(self.own, paired, middle_near)


class Scan:
    def __init__(self, order, memory, normer, later):
        self.order, self.later = order, later
        self.heads = normer.shape[0]
        self.total = jnp.concatenate(
            [memory.reshape(self.heads * HD, HD), jnp.pad(normer, ((0, 16 - self.heads), (0, 0)))]
        )
        self.before = jnp.zeros_like(self.total)
        self.bits = [2**k for k in range(lax.axis_size("dp").bit_length() - 1)]
        self.sent = flip(self.total.astype(bf16), self.bits[0])

    def step(self):
        bit = self.bits.pop(0)
        received = self.order.place(self.sent).astype(f32)
        place = lax.axis_index("dp")
        mine = (place & bit) == 0 if self.later else (place & bit) != 0
        self.before = self.before + jnp.where(mine, received, 0.0)
        if self.bits:
            self.total = self.order.done(self.total + received)
            self.sent = flip(self.total.astype(bf16), self.bits[0])

    def finish(self):
        while self.bits:
            self.step()
        rows = self.heads * HD
        memory = self.before[:rows].reshape(self.heads, HD, HD)
        return memory, self.before[rows : rows + self.heads]


LIMIT = 56 * 1024 * 1024


def params():
    return pltpu.CompilerParams(vmem_limit_bytes=LIMIT)


def cost(flops, moved):
    return pl.CostEstimate(flops=flops // 64, bytes_accessed=moved // 64, transcendentals=0)


def whole_block(shape):
    return pl.BlockSpec(shape, lambda *_: (0,) * len(shape))


def dot(left_side, right_side, left_dim=1, right_dim=0, precision=None):
    return lax.dot_general(
        left_side,
        right_side,
        (((left_dim,), (right_dim,)), ((), ())),
        precision=precision,
        preferred_element_type=f32,
    )


def feature(values):
    return jnp.where(values > 0, values + 1.0, jnp.exp(jnp.minimum(values, 0.0)))


def slope(values):
    return jnp.where(values > 0, 1.0, jnp.exp(jnp.minimum(values, 0.0)))


def qkv_kernel(rows_ref, gain_ref, near_ref, far_ref, normed_ref, qkv_ref):
    half = rows_ref.shape[1] // 2

    @pl.when(pl.program_id(0) == 0)
    def _():
        rows = rows_ref[...].astype(f32)
        scale = lax.rsqrt(jnp.mean(rows * rows, axis=-1, keepdims=True) + epsilon)
        normed_ref[...] = (rows * scale * gain_ref[...]).astype(bf16)

    total = dot(normed_ref[:, :half], near_ref[...]) + dot(normed_ref[:, half:], far_ref[...])
    qkv_ref[...] = total.astype(bf16)


def norm_qkv(rows, gain, weight, columns, tile=512):
    seg, width = rows.shape
    return pl.pallas_call(
        qkv_kernel,
        grid=(columns // tile,),
        in_specs=[
            whole_block((seg, width)),
            whole_block((1, width)),
            pl.BlockSpec((width // 2, tile), lambda j: (0, j)),
            pl.BlockSpec((width // 2, tile), lambda j: (0, j)),
        ],
        out_specs=[whole_block((seg, width)), pl.BlockSpec((seg, tile), lambda j: (0, j))],
        out_shape=[
            jax.ShapeDtypeStruct((seg, width), bf16),
            jax.ShapeDtypeStruct((seg, columns), bf16),
        ],
        compiler_params=params(),
        cost_estimate=cost(2 * seg * width * columns, 2 * (2 * seg * width + (width + seg) * columns)),
    )(rows, gain[None], *weight)


def soft_rows(query, key, start):
    seg = query.shape[0]
    scores = dot(query, key, 1, 1) * float(HD) ** (-0.5)
    at_q = lax.broadcasted_iota(jnp.int32, (seg, seg), 0)
    at_k = lax.broadcasted_iota(jnp.int32, (seg, seg), 1)
    in_q = (at_q >= start) & (at_q < start + PIECE)
    in_k = (at_k >= start) & (at_k < start + PIECE)
    scores = jnp.where((at_k <= at_q) | (in_q & in_k), scores, -1e30)
    raised = jnp.exp(scores - jnp.max(scores, axis=-1, keepdims=True))
    return raised / jnp.sum(raised, axis=-1, keepdims=True)


def memory_kernel(key_ref, value_ref, memory_ref, normer_ref):
    feature_k = feature(key_ref[...].astype(f32))
    memory_ref[0] = dot(feature_k, value_ref[...].astype(f32), 0, 0, highest)
    normer_ref[0] = jnp.broadcast_to(jnp.sum(feature_k, axis=0, keepdims=True), normer_ref.shape[1:])


def local_kernel(start_ref, query_ref, key_ref, value_ref, mix_ref):
    soft = soft_rows(query_ref[...], key_ref[...], start_ref[0])
    mix_ref[...] = dot(soft.astype(bf16), value_ref[...])


def head_block(seg, heads, part):
    return pl.BlockSpec((seg, HD), lambda h: (0, part * heads + h))


def segment_memory(qkv, heads):
    seg = qkv.shape[0]
    memory, normer = pl.pallas_call(
        memory_kernel,
        grid=(heads,),
        in_specs=[head_block(seg, heads, 1), head_block(seg, heads, 2)],
        out_specs=[
            pl.BlockSpec((1, HD, HD), lambda h: (h, 0, 0)),
            pl.BlockSpec((1, 8, HD), lambda h: (h, 0, 0)),
        ],
        out_shape=[
            jax.ShapeDtypeStruct((heads, HD, HD), f32),
            jax.ShapeDtypeStruct((heads, 8, HD), f32),
        ],
        compiler_params=params(),
        cost_estimate=cost(12 * seg * heads * HD * HD, 4 * seg * heads * HD),
    )(qkv, qkv)
    return memory, normer[:, 0]


def local_attention(qkv, start, heads):
    seg = qkv.shape[0]
    return pl.pallas_call(
        local_kernel,
        grid=(heads,),
        in_specs=[pl.BlockSpec(memory_space=pltpu.SMEM)]
        + [head_block(seg, heads, part) for part in range(3)],
        out_specs=pl.BlockSpec((seg, HD), lambda h: (0, h)),
        out_shape=jax.ShapeDtypeStruct((seg, heads * HD), f32),
        compiler_params=params(),
        cost_estimate=cost(40 * seg * seg * heads * HD, 10 * seg * heads * HD),
    )(start, qkv, qkv, qkv)


def recall(query, memory, normer):
    feature_q = feature(query.astype(f32))
    denominator = jnp.sum(feature_q * normer, axis=-1, keepdims=True) + 1.0
    inverse = 1.0 / denominator
    return feature_q, inverse, dot(feature_q, memory, 1, 0, highest) * inverse


def mix_kernel(gate_ref, query_ref, mix_ref, memory_ref, normer_ref, near_ref, far_ref, heads_ref, out_ref):
    heads = memory_ref.shape[0]
    half = near_ref.shape[1]
    for h in range(heads):
        columns = slice(h * HD, (h + 1) * HD)
        gate = gate_ref[h]
        _, _, recalled = recall(query_ref[:, columns], memory_ref[h], normer_ref[h : h + 1])
        mixture = gate * recalled + (1.0 - gate) * mix_ref[:, columns]
        heads_ref[:, columns] = mixture.astype(bf16)
    out_ref[:, :half] = dot(heads_ref[...], near_ref[...]).astype(bf16)
    out_ref[:, half:] = dot(heads_ref[...], far_ref[...]).astype(bf16)


def mix_and_project(gate, qkv, local_mix, memory, normer, weight):
    seg, inner = local_mix.shape
    width = 2 * weight[0].shape[1]
    return pl.pallas_call(
        mix_kernel,
        grid=(1,),
        in_specs=[
            pl.BlockSpec(memory_space=pltpu.SMEM),
            whole_block((seg, inner)),
            whole_block((seg, inner)),
            whole_block(memory.shape),
            whole_block(normer.shape),
            whole_block(weight[0].shape),
            whole_block(weight[1].shape),
        ],
        out_specs=[whole_block((seg, inner)), whole_block((seg, width))],
        out_shape=[
            jax.ShapeDtypeStruct((seg, inner), bf16),
            jax.ShapeDtypeStruct((seg, width), bf16),
        ],
        compiler_params=params(),
        cost_estimate=cost(2 * seg * inner * (width + 6 * HD), 8 * seg * inner + 2 * (seg + inner) * width),
    )(gate, qkv, local_mix, memory, normer, *weight)


def act_kernel(
    normed_ref, cot_ref, gate_near, gate_far, up_near, up_far, down_near, down_far,
    act_ref, gate_grad_ref, up_grad_ref,
):
    half = normed_ref.shape[1] // 2
    near, far = normed_ref[:, :half], normed_ref[:, half:]
    gated = dot(near, gate_near[...]) + dot(far, gate_far[...])
    upper = dot(near, up_near[...]) + dot(far, up_far[...])
    act_grad = dot(cot_ref[:, :half], down_near[...], 1, 1) + dot(cot_ref[:, half:], down_far[...], 1, 1)
    gate = jax.nn.sigmoid(gated)
    swish = gated * gate
    act_ref[...] = (swish * upper).astype(bf16)
    gate_grad_ref[...] = (act_grad * upper * (gate * (1.0 + gated * (1.0 - gate)))).astype(bf16)
    up_grad_ref[...] = (act_grad * swish).astype(bf16)


def activations(normed, cot, gate, up, down, tile):
    seg, width = normed.shape
    hidden = down[0].shape[0]
    half = width // 2
    into = pl.BlockSpec((half, tile), lambda j: (0, j))
    back = pl.BlockSpec((tile, half), lambda j: (j, 0))
    out = pl.BlockSpec((seg, tile), lambda j: (0, j))
    return pl.pallas_call(
        act_kernel,
        grid=(hidden // tile,),
        in_specs=[whole_block((seg, width))] * 2 + [into] * 4 + [back] * 2,
        out_specs=[out] * 3,
        out_shape=[jax.ShapeDtypeStruct((seg, hidden), bf16)] * 3,
        compiler_params=params(),
        cost_estimate=cost(6 * seg * width * hidden, 6 * hidden * width + 4 * seg * width + 6 * seg * hidden),
    )(normed, cot, *gate, *up, *down)


def width_kernel(weight_dim, count, *refs):
    lefts, weights, out_ref = refs[:count], refs[count:-1], refs[-1]
    half = out_ref.shape[1] // 2
    tile = weights[0].shape[1 - weight_dim]
    for place in range(2):
        total = dot(lefts[0][...], weights[place][...], 1, weight_dim)
        for k in range(1, count):
            total = total + dot(lefts[k][...], weights[2 * k + place][...], 1, weight_dim)
        start = pl.multiple_of(place * half + pl.program_id(0) * tile, tile)
        out_ref[:, pl.ds(start, tile)] = total.astype(bf16)


def into_width(lefts, weights, weight_dim, tile=256):
    seg, inner = lefts[0].shape
    half = weights[0][0].shape[1 - weight_dim]
    shape = (inner, tile) if weight_dim == 0 else (tile, inner)
    block = pl.BlockSpec(shape, lambda j: (0, j) if weight_dim == 0 else (j, 0))
    count = len(lefts)
    return pl.pallas_call(
        functools.partial(width_kernel, weight_dim, count),
        grid=(half // tile,),
        in_specs=[whole_block((seg, inner))] * count + [block] * (2 * count),
        out_specs=whole_block((seg, 2 * half)),
        out_shape=jax.ShapeDtypeStruct((seg, 2 * half), bf16),
        compiler_params=params(),
        cost_estimate=cost(
            4 * count * seg * inner * half, count * (2 * seg * inner + 4 * inner * half) + 4 * seg * half
        ),
    )(*lefts, *[half_weight for weight in weights for half_weight in weight])


def recall_grad_kernel(
    gate_ref, keep_ref, mid_ref, near_ref, far_ref, query_ref, mix_ref, memory_ref, normer_ref,
    local_ref, query_grad_ref, memory_grad_ref, normer_grad_ref, gate_grad_ref,
):
    h = pl.program_id(0)
    half = near_ref.shape[1]
    gate = gate_ref[h]
    keep = keep_ref[0]
    mixture_grad = dot(mid_ref[:, :half], near_ref[...], 1, 1) + dot(mid_ref[:, half:], far_ref[...], 1, 1)
    normer = normer_ref[0, :1]
    feature_q, inverse, recalled = recall(query_ref[...], memory_ref[0], normer)
    gate_grad_ref[0] = jnp.broadcast_to(
        jnp.sum(mixture_grad * (recalled - mix_ref[...]), axis=0, keepdims=True), gate_grad_ref.shape[1:]
    )
    local_ref[...] = ((1.0 - gate) * mixture_grad).astype(bf16)
    share = gate * mixture_grad * inverse
    weigh = jnp.sum(share * recalled, axis=-1, keepdims=True)
    memory_grad_ref[0] = dot(feature_q, share, 0, 0, highest) * keep
    normer_grad_ref[0] = jnp.broadcast_to(
        -jnp.sum(weigh * feature_q, axis=0, keepdims=True) * keep, normer_grad_ref.shape[1:]
    )
    query_grad_ref[...] = (dot(share, memory_ref[0], 1, 1, highest) - weigh * normer) * slope(
        query_ref[...].astype(f32)
    )


def recall_backward(gate, keep, mid_seg, weight, qkv, local_mix, memory, normer):
    seg, width = mid_seg.shape
    heads = memory.shape[0]
    half = width // 2
    columns = pl.BlockSpec((seg, HD), lambda h: (0, h))
    row_block = pl.BlockSpec((1, 8, HD), lambda h: (h, 0, 0))
    memory_block = pl.BlockSpec((1, HD, HD), lambda h: (h, 0, 0))
    normer_rows = jnp.broadcast_to(normer[:, None], (heads, 8, HD))
    local_grad, query_grad, memory_grad, normer_grad, gate_grad = pl.pallas_call(
        recall_grad_kernel,
        grid=(heads,),
        in_specs=[
            pl.BlockSpec(memory_space=pltpu.SMEM),
            pl.BlockSpec(memory_space=pltpu.SMEM),
            whole_block((seg, width)),
            pl.BlockSpec((HD, half), lambda h: (h, 0)),
            pl.BlockSpec((HD, half), lambda h: (h, 0)),
            columns,
            columns,
            memory_block,
            row_block,
        ],
        out_specs=[columns, columns, memory_block, row_block, row_block],
        out_shape=[
            jax.ShapeDtypeStruct((seg, heads * HD), bf16),
            jax.ShapeDtypeStruct((seg, heads * HD), f32),
            jax.ShapeDtypeStruct((heads, HD, HD), f32),
            jax.ShapeDtypeStruct((heads, 8, HD), f32),
            jax.ShapeDtypeStruct((heads, 8, HD), f32),
        ],
        compiler_params=params(),
        cost_estimate=cost(2 * seg * heads * HD * (width + 12 * HD), 2 * seg * width + 12 * seg * heads * HD),
    )(gate, keep, mid_seg, *weight, qkv, local_mix, memory, normer_rows)
    return local_grad, query_grad, memory_grad, normer_grad[:, 0], jnp.sum(gate_grad[:, 0], axis=-1)


def local_grad_kernel(
    start_ref, query_ref, key_ref, value_ref, local_ref, extra_ref, query_grad_ref, key_grad_ref, value_grad_ref
):
    scale = float(HD) ** (-0.5)
    query, key, local = query_ref[...], key_ref[...], local_ref[...]
    soft = soft_rows(query, key, start_ref[0])
    value_grad_ref[...] = dot(soft.astype(bf16), local, 0, 0)
    prob_grad = dot(local, value_ref[...], 1, 1)
    score_grad = (soft * (prob_grad - jnp.sum(soft * prob_grad, axis=-1, keepdims=True))).astype(bf16)
    query_grad_ref[...] = (dot(score_grad, key) * scale + extra_ref[...]).astype(bf16)
    key_grad_ref[...] = dot(score_grad, query, 0, 0) * scale


def local_backward(start, qkv, local_grad, query_extra, heads):
    seg = qkv.shape[0]
    columns = pl.BlockSpec((seg, HD), lambda h: (0, h))
    return pl.pallas_call(
        local_grad_kernel,
        grid=(heads,),
        in_specs=[pl.BlockSpec(memory_space=pltpu.SMEM)]
        + [head_block(seg, heads, part) for part in range(3)]
        + [columns, columns],
        out_specs=[columns, columns, columns],
        out_shape=[
            jax.ShapeDtypeStruct((seg, heads * HD), bf16),
            jax.ShapeDtypeStruct((seg, heads * HD), f32),
            jax.ShapeDtypeStruct((seg, heads * HD), f32),
        ],
        compiler_params=params(),
        cost_estimate=cost(80 * seg * seg * heads * HD, 20 * seg * heads * HD),
    )(start, qkv, qkv, qkv, local_grad, query_extra)


def back_kernel(
    rows_ref, qkv_ref, query_grad_ref, key_grad_ref, value_grad_ref, memory_ref, normer_ref,
    near_ref, far_ref, grads_ref, part_ref, gain_ref,
):
    heads = memory_ref.shape[0]
    inner = heads * HD
    half = near_ref.shape[0]
    grads_ref[:, :inner] = query_grad_ref[...]
    for h in range(heads):
        columns = slice(h * HD, (h + 1) * HD)
        key = qkv_ref[:, inner + h * HD : inner + (h + 1) * HD].astype(f32)
        value = qkv_ref[:, 2 * inner + h * HD : 2 * inner + (h + 1) * HD].astype(f32)
        key_extra = dot(value, memory_ref[h], 1, 1, highest) + normer_ref[h : h + 1]
        grads_ref[:, inner + h * HD : inner + (h + 1) * HD] = (
            key_grad_ref[:, columns] + key_extra * slope(key)
        ).astype(bf16)
        grads_ref[:, 2 * inner + h * HD : 2 * inner + (h + 1) * HD] = (
            value_grad_ref[:, columns] + dot(feature(key), memory_ref[h], 1, 0, highest)
        ).astype(bf16)
    rows = rows_ref[...].astype(f32)
    scale = lax.rsqrt(jnp.mean(rows * rows, axis=-1, keepdims=True) + epsilon)
    for place, weight_ref in enumerate((near_ref, far_ref)):
        columns = slice(place * half, (place + 1) * half)
        part = dot(grads_ref[...], weight_ref[...], 1, 1)
        part_ref[:, columns] = part.astype(bf16)
        gain_ref[:, columns] = jnp.broadcast_to(
            jnp.sum(part * (rows[:, columns] * scale), axis=0, keepdims=True), (8, half)
        )


def attention_back(rows, qkv, query_grad, key_grad, value_grad, memory, normer, weight):
    seg, width = rows.shape
    columns = qkv.shape[1]
    inner = columns // 3
    grads, part, gain = pl.pallas_call(
        back_kernel,
        grid=(1,),
        in_specs=[
            whole_block((seg, width)),
            whole_block((seg, columns)),
            whole_block((seg, inner)),
            whole_block((seg, inner)),
            whole_block((seg, inner)),
            whole_block(memory.shape),
            whole_block(normer.shape),
            whole_block((width // 2, columns)),
            whole_block((width // 2, columns)),
        ],
        out_specs=[whole_block((seg, columns)), whole_block((seg, width)), whole_block((8, width))],
        out_shape=[
            jax.ShapeDtypeStruct((seg, columns), bf16),
            jax.ShapeDtypeStruct((seg, width), bf16),
            jax.ShapeDtypeStruct((8, width), f32),
        ],
        compiler_params=params(),
        cost_estimate=cost(2 * seg * columns * (width + 4 * HD), 2 * (width * columns + 2 * seg * width + 3 * seg * columns)),
    )(rows, qkv, query_grad, key_grad, value_grad, memory, normer, *weight)
    return grads, part, gain[0]


def grad_kernel(count, has_more, *refs):
    lefts, rights = refs[:count], refs[count : 2 * count]
    total = dot(lefts[0][...], rights[0][...], 0, 0)
    for left, right in zip(lefts[1:], rights[1:]):
        total = total + dot(left[...], right[...], 0, 0)
    if has_more:
        total = total + refs[2 * count][...].astype(f32)
    refs[-1][...] = total.astype(refs[-1].dtype)


def grad_product(lefts, rights, left_part, right_part, more=None, tile_i=256, tile_j=2048):
    seg = lefts[0].shape[0]
    height = lefts[0].shape[1] // left_part[1]
    length = rights[0].shape[1] // right_part[1]
    tile_i, tile_j = min(tile_i, height), min(tile_j, length)
    base_i, base_j = left_part[0] * (height // tile_i), right_part[0] * (length // tile_j)
    out_block = pl.BlockSpec((tile_i, tile_j), lambda i, j: (i, j))
    return pl.pallas_call(
        functools.partial(grad_kernel, len(lefts), more is not None),
        grid=(height // tile_i, length // tile_j),
        in_specs=[pl.BlockSpec((seg, tile_i), lambda i, j: (0, base_i + i)) for _ in lefts]
        + [pl.BlockSpec((seg, tile_j), lambda i, j: (0, base_j + j)) for _ in rights]
        + ([] if more is None else [out_block]),
        out_specs=out_block,
        out_shape=jax.ShapeDtypeStruct((height, length), bf16),
        compiler_params=params(),
        cost_estimate=cost(
            2 * len(lefts) * seg * height * length,
            2 * len(lefts) * seg * (height + length) + 4 * height * length,
        ),
    )(*lefts, *rights, *([] if more is None else [more]))


def inverse_rms(values):
    return lax.rsqrt(jnp.mean(values * values, axis=-1, keepdims=True) + epsilon)


def norm_pull(values, scale, gain, grad):
    weighted = gain * grad
    return scale * (
        weighted - values * (scale * scale) * jnp.mean(weighted * values, axis=-1, keepdims=True)
    )


def weight_grad(order, left_sides, right_sides, axis):
    def product(place, more=None):
        part = (place, 2)
        return grad_product(
            [order.place(left_sides[0]), *left_sides[1:]],
            right_sides,
            part if axis == 0 else (0, 1),
            part if axis == 1 else (0, 1),
            more,
        )

    return Collect(order, product, axis)


def on_device(
    hidden_in,
    out_cotangent,
    piece_start,
    query_weight,
    key_weight,
    value_weight,
    output_weight,
    gate_weight,
    up_weight,
    down_weight,
    attn_gain,
    mlp_gain,
    memory_gate,
):
    dp_index = lax.axis_index("dp")
    dp_count = lax.axis_size("dp")
    tensor_count = lax.axis_size("tensor")
    heads_here = memory_gate.shape[0]
    width = hidden_in.shape[2]
    blocks = half_order(dp_count)
    tile = 512
    order = Order()

    inward_table, outward_table = tables(dp_index, blocks)
    gate_sig = jax.nn.sigmoid(memory_gate)
    keep = jnp.where(dp_index == 0, 0.0, 1.0).astype(f32)[None]
    gain_columns = jnp.pad(jnp.stack([attn_gain, mlp_gain], axis=1), ((0, 0), (0, HD - 2)))
    qkvg = jnp.concatenate([query_weight, key_weight, value_weight, gain_columns], axis=1)
    qkv_width = qkvg.shape[1] - HD
    one = SimpleNamespace()
    two = SimpleNamespace()

    one.rows, two.rows = move_columns([hidden_in[0], hidden_in[1]], inward_table)
    order.done(one.rows)
    rows_one = OffloadGather(order, one.rows)
    rows_two = OffloadGather(order, two.rows)
    qkvg_spread = Spread(order, qkvg, 0)
    one.cot, two.cot = move_columns(
        [order.place(out_cotangent[0]), out_cotangent[1]], inward_table
    )
    order.done(one.cot)
    qkvg_spread.second()
    output_spread = Spread(order, output_weight, 1)
    qkvg_spread.third()
    one.rows_seg = rows_one.finish()

    gains = jnp.concatenate(
        [half[:, qkv_width : qkv_width + 2] for half in qkvg_spread.whole], axis=0
    )
    gains = jnp.transpose(gains.astype(f32))
    gain_one, gain_two = gains[0], gains[1]

    def project(now):
        now.seg_in, now.qkv = norm_qkv(
            order.place(now.rows_seg), gain_one, qkvg_spread.whole, qkv_width
        )
        order.done(now.qkv)

    def remember(now):
        memory, normer = segment_memory(order.place(now.qkv), heads_here)
        order.done(memory)
        now.scan = Scan(order, memory, normer, False)

    def attend(now, b):
        now.mix = local_attention(order.place(now.qkv), piece_start[b], heads_here)
        order.done(now.mix)

    def mix(now):
        now.memory, now.normer = now.scan.finish()
        now.heads_out, part = mix_and_project(
            gate_sig, order.place(now.qkv), now.mix, now.memory, now.normer,
            output_spread.whole,
        )
        order.done(now.heads_out)
        now.scatter = OffloadScatter(order, part)

    def norm_middle(now):
        now.middle = now.rows.astype(f32) + now.scatter.finish()
        now.scale_two = inverse_rms(now.middle)
        normed = (now.middle * now.scale_two * gain_two).astype(bf16)
        now.gather = OffloadGather(order, order.done(normed))

    def activate(now):
        now.act, now.gate_grad, now.up_grad = activations(
            order.place(now.seg_two), now.cot_seg, gate_spread.whole, up_spread.whole,
            down_spread.whole, tile,
        )
        order.done(now.act)

    def feed_back(now):
        part = into_width(
            [order.place(now.gate_grad), now.up_grad], [gate_spread.whole, up_spread.whole], 1
        )
        now.scatter = OffloadScatter(order, order.done(part))

    def feed_rows(now):
        part = into_width([order.place(now.act)], [down_spread.whole], 0)
        now.feed_rows = OffloadScatter(order, order.done(part))

    def norm_out(now):
        rows = now.feed_rows.finish()
        now.hidden_out = order.done((now.middle + rows).astype(bf16))

    def norm_grad(now):
        grad = now.scatter.finish()
        middle, scale = now.middle, now.scale_two
        now.gain_two_term = jnp.sum(grad * middle * scale, axis=0)
        now.middle_grad = now.cot.astype(f32) + norm_pull(middle, scale, gain_two, grad)
        now.gather = OffloadGather(order, order.done(now.middle_grad.astype(bf16)))

    def recall_back(now):
        local_grad, query_extra, memory_grad, normer_grad, now.gate_term = recall_backward(
            gate_sig, keep, order.place(now.mid_seg), output_spread.whole, now.qkv,
            now.mix, now.memory, now.normer,
        )
        now.local = order.done(local_grad), query_extra
        now.scan = Scan(order, memory_grad, normer_grad, True)

    def local_back(now, b):
        now.grads = local_backward(
            piece_start[b], order.place(now.qkv), *now.local, heads_here
        )
        order.done(now.grads[0])

    def attention_backward(now):
        now.qkv_grad, part, now.gain_one_term = attention_back(
            order.place(now.rows_seg), now.qkv, *now.grads, *now.scan.finish(),
            qkvg_spread.whole,
        )
        order.done(now.qkv_grad)
        now.scatter = OffloadScatter(order, part)

    def norm_in_grad(now):
        own_rows = now.rows.astype(f32)
        now.hidden_grad = order.done(
            now.middle_grad
            + norm_pull(own_rows, inverse_rms(own_rows), gain_one, now.scatter.finish())
        )

    def small_messages():
        gate_sum = (one.gate_term + two.gate_term) * gate_sig * (1.0 - gate_sig)
        halves_here = len(blocks)
        half_width = width // halves_here
        by_half = [term.reshape(halves_here, half_width) for term in (one.gain_one_term + two.gain_one_term, one.gain_two_term + two.gain_two_term)]
        messages = []
        for offset in range(dp_count):
            pick = [blocks.index((offset, half)) for half in range(2)]
            message = jnp.concatenate(
                [term[k] for term in by_half for k in pick] + [jnp.pad(gate_sum, (0, HD - heads_here))]
            )
            messages.append(flip(message, offset) if offset else message)
        return messages

    project(one)
    output_spread.second()
    remember(one)
    attend(one, 0)
    one.scan.step()
    output_spread.third()
    one.scan.step()
    mix(one)
    gate_spread = Spread(order, gate_weight, 0)
    two.rows_seg = rows_two.finish()
    cot_one = Gather(order, one.cot)
    project(two)
    remember(two)
    attend(two, 1)
    two.scan.step()
    cot_one.second()
    two.scan.step()
    mix(two)
    cot_one.third()
    up_spread = Spread(order, up_weight, 0)
    norm_middle(one)
    cot_two = Gather(order, two.cot)
    gate_spread.second()
    one.cot_seg = cot_one.finish()
    up_spread.second()
    cot_two.second()
    gate_spread.third()
    down_spread = Spread(order, down_weight, 1)
    cot_two.third()
    norm_middle(two)
    up_spread.third()
    down_spread.second()
    two.cot_seg = cot_two.finish()
    down_spread.third()
    one.seg_two = one.gather.finish()

    activate(one)
    feed_back(one)
    two.seg_two = two.gather.finish()
    activate(two)
    feed_back(two)
    gate_collect = weight_grad(order, [one.seg_two, two.seg_two], [one.gate_grad, two.gate_grad], 0)
    norm_grad(one)
    up_collect = weight_grad(order, [one.seg_two, two.seg_two], [one.up_grad, two.up_grad], 0)
    down_collect = weight_grad(order, [one.act, two.act], [one.cot_seg, two.cot_seg], 1)
    norm_grad(two)
    gate_collect.second()
    up_collect.second()

    one.mid_seg = one.gather.finish()
    recall_back(one)
    local_back(one, 0)
    one.scan.step()
    one.scan.step()
    attention_backward(one)
    two.mid_seg = two.gather.finish()
    recall_back(two)
    local_back(two, 1)
    two.scan.step()
    two.scan.step()
    attention_backward(two)
    feed_rows(one)
    gate_collect.third()
    down_collect.second()
    qkv_collect = weight_grad(order, [one.seg_in, two.seg_in], [one.qkv_grad, two.qkv_grad], 0)
    up_collect.third()
    feed_rows(two)
    qkv_collect.second()
    gate_total = gate_collect.finish()
    output_collect = weight_grad(order, [one.heads_out, two.heads_out], [one.mid_seg, two.mid_seg], 1)
    norm_in_grad(one)
    down_collect.third()
    output_collect.second()
    up_total = up_collect.finish()
    qkv_collect.third()
    messages = order.place(small_messages())
    norm_in_grad(two)
    down_grad = down_collect.finish()
    output_collect.third()
    norm_out(one)
    output_grad = output_collect.finish()
    norm_out(two)
    qkv_total = qkv_collect.finish()
    block = width // dp_count
    small_sum = sum(order.place(messages))
    gain_part = small_sum[: 2 * block]
    gain_sum = gain_part
    for hop in range(1, tensor_count):
        gain_sum = gain_sum + send(
            gain_part, [(i, (i + hop) % tensor_count) for i in range(tensor_count)]
        )

    query_total, key_total, value_total = cut(qkv_total, 3, 1)
    return (
        move_columns([jnp.stack([one.hidden_out, two.hidden_out])], outward_table)[0],
        move_columns([jnp.stack([one.hidden_grad, two.hidden_grad])], outward_table)[0],
        query_total,
        key_total,
        value_total,
        output_grad,
        gate_total,
        up_total,
        down_grad,
        gain_sum[:block],
        gain_sum[block:],
        small_sum[2 * block : 2 * block + heads_here],
    )


def solution(mesh):
    rows = P(None, ("dp", "tensor"))
    inward = P("dp", "tensor")
    outward = P("tensor", "dp")
    return jax.shard_map(
        on_device,
        mesh=mesh,
        in_specs=(
            rows, rows, P(None, "dp"), inward, inward, inward, outward, inward, inward, outward,
            P("dp"), P("dp"), P("tensor"),
        ),
        out_specs=(
            rows, rows, inward, inward, inward, outward, inward, inward, outward,
            P("dp"), P("dp"), P("tensor"),
        ),
        check_vma=False,
    )
```

```python
import functools
from types import SimpleNamespace

import jax
import jax.numpy as jnp
from jax import lax
from jax.experimental import pallas as pl
from jax.experimental.pallas import tpu as pltpu
from jax.sharding import PartitionSpec as P

HD = 128
PIECE = 256
epsilon = 1e-05
highest = lax.Precision.HIGHEST
bf16 = jnp.bfloat16
f32 = jnp.float32


class Order:
    def __init__(self):
        self.last = None

    def place(self, values):
        if self.last is None:
            return values
        return lax.optimization_barrier((values, self.last))[0]

    def done(self, values):
        self.last = values
        return values


NEAR = [(0, 0), (0, 1), (2, 1), (2, 0), (6, 0), (6, 1), (4, 1), (4, 0)]


def far_bits(count):
    bits = [1]
    while 2 ** (2 + len(bits)) < count:
        bits.append(2 ** (2 + len(bits)))
    return bits


def half_order(count):
    order = list(NEAR)
    for bit in far_bits(count):
        order = order + [(offset | bit, half) for offset, half in order]
    return order


def flip(values, bit):
    count = lax.axis_size("dp")
    return lax.ppermute(values, "dp", [(i, i ^ bit) for i in range(count)])


def cut(values, parts, axis):
    size = values.shape[axis] // parts
    return [lax.slice_in_dim(values, k * size, (k + 1) * size, axis=axis) for k in range(parts)]


def join_kernel(axis, own_ref, a_ref, b_ref, far_0_ref, far_1_ref, out_ref):
    size = far_0_ref.shape[axis]

    def part(ref, place, count=1):
        where = slice(place * size, (place + count) * size)
        return (where, slice(None)) if axis == 0 else (slice(None), where)

    out_ref[part(out_ref, 0, 2)] = own_ref[...]
    out_ref[part(out_ref, 2)] = a_ref[part(a_ref, 1)]
    out_ref[part(out_ref, 3)] = a_ref[part(a_ref, 0)]
    out_ref[part(out_ref, 4)] = far_0_ref[...]
    out_ref[part(out_ref, 5)] = far_1_ref[...]
    out_ref[part(out_ref, 6)] = b_ref[part(b_ref, 1)]
    out_ref[part(out_ref, 7)] = b_ref[part(b_ref, 0)]


def join_blocks(own, near_a, near_b, far_0, far_1, axis):
    if axis == 1 and far_0.shape[1] % HD:
        a, b = cut(near_a, 2, axis), cut(near_b, 2, axis)
        return jnp.concatenate([own, a[1], a[0], far_0, far_1, b[1], b[0]], axis=axis)
    other = 1 - axis
    parts = 4 if own.shape[other] % (4 * HD) == 0 else 1
    shape = list(own.shape)
    shape[axis] *= 4

    def block(dims):
        dims = list(dims)
        dims[other] //= parts
        return pl.BlockSpec(tuple(dims), lambda j: (0, j) if axis == 0 else (j, 0))

    arrays = (own, near_a, near_b, far_0, far_1)
    return pl.pallas_call(
        functools.partial(join_kernel, axis),
        grid=(parts,),
        in_specs=[block(array.shape) for array in arrays],
        out_specs=block(shape),
        out_shape=jax.ShapeDtypeStruct(tuple(shape), own.dtype),
        compiler_params=params(),
        cost_estimate=cost(64, 64),
    )(*arrays)


class Spread:
    def __init__(self, order, own, axis):
        self.order, self.axis = order, axis
        self.own = order.place(own)
        self.near_a, self.near_b = flip(self.own, 2), flip(self.own, 4)

    def second(self):
        self.near_a, self.near_b = self.order.done(self.order.place((self.near_a, self.near_b)))
        b_0 = cut(self.near_b, 2, self.axis)[0]
        a_1 = cut(self.near_a, 2, self.axis)[1]
        self.far = flip(b_0, 2), flip(a_1, 4)

    def third(self):
        far = self.order.place(self.far)
        known = self.order.done(join_blocks(self.own, self.near_a, self.near_b, *far, self.axis))
        bits = far_bits(lax.axis_size("dp"))
        for bit in bits[:-1]:
            known = jnp.concatenate([known, flip(known, bit)], axis=self.axis)
        self.whole = known, flip(known, bits[-1])

    def arrive(self):
        self.whole = self.order.done(self.order.place(self.whole))


def plus(*terms):
    total = terms[0].astype(f32)
    for term in terms[1:]:
        total = total + term.astype(f32)
    return total


class Collect:
    def __init__(self, order, product, axis):
        self.order, self.product, self.axis = order, product, axis
        self.bits = far_bits(lax.axis_size("dp"))
        product_two = order.done(product(1))
        self.received = flip(product_two, self.bits[-1])

    def second(self):
        total = self.order.done(self.product(0, self.received))
        axis = self.axis
        for bit in reversed(self.bits[:-1]):
            one, two = cut(total, 2, axis)
            total = plus(one, flip(two, bit)).astype(bf16)
        self.parts = cut(total, 8, axis)
        size = self.parts[0].shape[axis]
        self.got_x = flip(lax.slice_in_dim(total, 3 * size, 5 * size, axis=axis), 2)
        self.got_y = flip(lax.slice_in_dim(total, 5 * size, 7 * size, axis=axis), 4)

    def third(self):
        got_x, got_y = self.order.place((self.got_x, self.got_y))
        self.mine_x, pass_x = cut(got_x, 2, self.axis)
        pass_y, self.mine_y = cut(got_y, 2, self.axis)
        go_x = plus(self.parts[2], pass_y).astype(bf16)
        go_y = plus(self.parts[7], pass_x).astype(bf16)
        go_x, go_y = self.order.done((go_x, go_y))
        self.last_x, self.last_y = flip(go_x, 2), flip(go_y, 4)

    def finish(self):
        self.last_x, self.last_y = self.order.place((self.last_x, self.last_y))
        return self.order.done(
            jnp.concatenate(
                [
                    plus(self.parts[0], self.mine_x, self.last_y),
                    plus(self.parts[1], self.last_x, self.mine_y),
                ],
                axis=self.axis,
            )
        )


def move_kernel(table_ref, *refs):
    count = len(refs) // 2
    pieces = table_ref.shape[0]
    width = refs[0].shape[-1] // pieces
    for source, target in zip(refs[:count], refs[count:]):
        for k in range(pieces):
            start = pl.multiple_of(table_ref[k] * width, width)
            target[..., k * width : (k + 1) * width] = source[..., pl.ds(start, width)]


def move_columns(arrays, table):
    width = arrays[0].shape[-1] // table.shape[0]
    if width % HD:
        return [
            jnp.concatenate(
                [
                    lax.dynamic_slice_in_dim(values, table[k] * width, width, axis=-1)
                    for k in range(table.shape[0])
                ],
                axis=-1,
            )
            for values in arrays
        ]
    vmem = pl.BlockSpec(memory_space=pltpu.VMEM)
    return pl.pallas_call(
        move_kernel,
        in_specs=[pl.BlockSpec(memory_space=pltpu.SMEM)] + [vmem for _ in arrays],
        out_specs=[vmem for _ in arrays],
        out_shape=[jax.ShapeDtypeStruct(values.shape, values.dtype) for values in arrays],
        compiler_params=pltpu.CompilerParams(vmem_limit_bytes=24 * 1024 * 1024),
    )(table, *arrays)


def tables(place, order):
    count = len(order) // 2
    inward = [[(own ^ offset) * 2 + half for offset, half in order] for own in range(count)]
    outward = [[row.index(block) for block in range(2 * count)] for row in inward]
    return [
        lax.dynamic_index_in_dim(jnp.asarray(table, jnp.int32), place, 0, False)
        for table in (inward, outward)
    ]


PAIRS = [(0, 1), (1, 0), (2, 3), (3, 2)]
MIDDLE = [(1, 2), (2, 1)]
OUTER = [(1, 0), (2, 3)]
INNER = [(0, 1), (3, 2)]


def send(values, pairs):
    return lax.ppermute(values, "tensor", pairs)


def at_end():
    place = lax.axis_index("tensor")
    return (place == 0) | (place == 3)


def slot_owner():
    place = lax.axis_index("tensor")
    low = place < 2
    return [place, place ^ 1, jnp.where(low, 2, 1), jnp.where(low, 3, 0)]


def offload_gather(own):
    return lax.all_gather(own, "tensor", axis=0, tiled=True)


class OffloadGather:
    def __init__(self, order, own):
        self.order = order
        self.whole = offload_gather(order.place(own))

    def finish(self):
        return self.whole


class OffloadScatter:
    def __init__(self, order, values):
        self.order = order
        self.own = lax.psum_scatter(values, "tensor", scatter_dimension=0, tiled=True)

    def finish(self):
        return self.order.place(self.own).astype(f32)


class Gather:
    def __init__(self, order, own):
        self.order = order
        self.own = order.place(own)
        self.partner = send(self.own, PAIRS)
        self.middle_near = send(self.own, MIDDLE)

    def second(self):
        self.partner, self.middle_near = self.order.done(
            self.order.place((self.partner, self.middle_near))
        )
        self.middle_far = send(self.partner, MIDDLE)
        self.outer_near = send(self.middle_near, OUTER)

    def third(self):
        self.middle_far, self.outer_near = self.order.done(
            self.order.place((self.middle_far, self.outer_near))
        )
        self.outer_far = send(self.middle_far, OUTER)

    def finish(self):
        outer_far = self.order.place(self.outer_far)
        end = at_end()
        near = jnp.where(end, self.outer_near, self.middle_near)
        far = jnp.where(end, outer_far, self.middle_far)
        rows = self.own.shape[0]
        whole = jnp.zeros((4 * rows, self.own.shape[1]), self.own.dtype)
        for owner, piece in zip(slot_owner(), (self.own, self.partner, near, far)):
            whole = lax.dynamic_update_slice_in_dim(whole, piece, owner * rows, axis=0)
        return self.order.done(whole)


class Scatter:
    def __init__(self, order, values):
        rows = values.shape[0] // 4
        self.order = order
        self.own, self.partner, self.near, self.far = [
            lax.dynamic_slice_in_dim(values, owner * rows, rows, axis=0) for owner in slot_owner()
        ]
        self.inner_far = send(self.far, INNER)
        self.inner_near = send(self.near, INNER)

    def second(self):
        go = self.order.done(plus(self.far, self.order.place(self.inner_far)).astype(bf16))
        self.middle_far = send(go, MIDDLE)

    def third(self):
        inner_near, middle_far = self.order.place((self.inner_near, self.middle_far))
        go_near = plus(self.near, inner_near).astype(bf16)
        go_pair = plus(self.partner, middle_far).astype(bf16)
        go_near, go_pair = self.order.done((go_near, go_pair))
        self.paired = send(go_pair, PAIRS)
        self.middle_near = send(go_near, MIDDLE)

    def finish(self):
        paired, middle_near = self.order.place((self.paired, self.middle_near))
        return plus(self.own, paired, middle_near)


class Scan:
    def __init__(self, order, memory, normer, later):
        self.order, self.later = order, later
        self.heads = normer.shape[0]
        self.total = jnp.concatenate(
            [memory.reshape(self.heads * HD, HD), jnp.pad(normer, ((0, 16 - self.heads), (0, 0)))]
        )
        self.before = jnp.zeros_like(self.total)
        self.bits = [2**k for k in range(lax.axis_size("dp").bit_length() - 1)]
        self.sent = flip(self.total.astype(bf16), self.bits[0])

    def step(self):
        bit = self.bits.pop(0)
        received = self.order.place(self.sent).astype(f32)
        place = lax.axis_index("dp")
        mine = (place & bit) == 0 if self.later else (place & bit) != 0
        self.before = self.before + jnp.where(mine, received, 0.0)
        if self.bits:
            self.total = self.order.done(self.total + received)
            self.sent = flip(self.total.astype(bf16), self.bits[0])

    def finish(self):
        while self.bits:
            self.step()
        rows = self.heads * HD
        memory = self.before[:rows].reshape(self.heads, HD, HD)
        return memory, self.before[rows : rows + self.heads]


LIMIT = 56 * 1024 * 1024


def params():
    return pltpu.CompilerParams(vmem_limit_bytes=LIMIT)


def cost(flops, moved):
    return pl.CostEstimate(flops=flops // 64, bytes_accessed=moved // 64, transcendentals=0)


def whole_block(shape):
    return pl.BlockSpec(shape, lambda *_: (0,) * len(shape))


def dot(left_side, right_side, left_dim=1, right_dim=0, precision=None):
    return lax.dot_general(
        left_side,
        right_side,
        (((left_dim,), (right_dim,)), ((), ())),
        precision=precision,
        preferred_element_type=f32,
    )


def feature(values):
    return jnp.where(values > 0, values + 1.0, jnp.exp(jnp.minimum(values, 0.0)))


def slope(values):
    return jnp.where(values > 0, 1.0, jnp.exp(jnp.minimum(values, 0.0)))


def qkv_kernel(rows_ref, gain_ref, near_ref, far_ref, normed_ref, qkv_ref):
    half = rows_ref.shape[1] // 2

    @pl.when(pl.program_id(0) == 0)
    def _():
        rows = rows_ref[...].astype(f32)
        scale = lax.rsqrt(jnp.mean(rows * rows, axis=-1, keepdims=True) + epsilon)
        normed_ref[...] = (rows * scale * gain_ref[...]).astype(bf16)

    total = dot(normed_ref[:, :half], near_ref[...]) + dot(normed_ref[:, half:], far_ref[...])
    qkv_ref[...] = total.astype(bf16)


def norm_qkv(rows, gain, weight, columns, tile=512):
    seg, width = rows.shape
    return pl.pallas_call(
        qkv_kernel,
        grid=(columns // tile,),
        in_specs=[
            whole_block((seg, width)),
            whole_block((1, width)),
            pl.BlockSpec((width // 2, tile), lambda j: (0, j)),
            pl.BlockSpec((width // 2, tile), lambda j: (0, j)),
        ],
        out_specs=[whole_block((seg, width)), pl.BlockSpec((seg, tile), lambda j: (0, j))],
        out_shape=[
            jax.ShapeDtypeStruct((seg, width), bf16),
            jax.ShapeDtypeStruct((seg, columns), bf16),
        ],
        compiler_params=params(),
        cost_estimate=cost(2 * seg * width * columns, 2 * (2 * seg * width + (width + seg) * columns)),
    )(rows, gain[None], *weight)


def soft_rows(query, key, start):
    seg = query.shape[0]
    scores = dot(query, key, 1, 1) * float(HD) ** (-0.5)
    at_q = lax.broadcasted_iota(jnp.int32, (seg, seg), 0)
    at_k = lax.broadcasted_iota(jnp.int32, (seg, seg), 1)
    in_q = (at_q >= start) & (at_q < start + PIECE)
    in_k = (at_k >= start) & (at_k < start + PIECE)
    scores = jnp.where((at_k <= at_q) | (in_q & in_k), scores, -1e30)
    raised = jnp.exp(scores - jnp.max(scores, axis=-1, keepdims=True))
    return raised / jnp.sum(raised, axis=-1, keepdims=True)


def memory_kernel(key_ref, value_ref, memory_ref, normer_ref):
    feature_k = feature(key_ref[...].astype(f32))
    memory_ref[0] = dot(feature_k, value_ref[...].astype(f32), 0, 0, highest)
    normer_ref[0] = jnp.broadcast_to(jnp.sum(feature_k, axis=0, keepdims=True), normer_ref.shape[1:])


def local_kernel(start_ref, query_ref, key_ref, value_ref, mix_ref):
    soft = soft_rows(query_ref[...], key_ref[...], start_ref[0])
    mix_ref[...] = dot(soft.astype(bf16), value_ref[...])


def head_block(seg, heads, part):
    return pl.BlockSpec((seg, HD), lambda h: (0, part * heads + h))


def segment_memory(qkv, heads):
    seg = qkv.shape[0]
    memory, normer = pl.pallas_call(
        memory_kernel,
        grid=(heads,),
        in_specs=[head_block(seg, heads, 1), head_block(seg, heads, 2)],
        out_specs=[
            pl.BlockSpec((1, HD, HD), lambda h: (h, 0, 0)),
            pl.BlockSpec((1, 8, HD), lambda h: (h, 0, 0)),
        ],
        out_shape=[
            jax.ShapeDtypeStruct((heads, HD, HD), f32),
            jax.ShapeDtypeStruct((heads, 8, HD), f32),
        ],
        compiler_params=params(),
        cost_estimate=cost(12 * seg * heads * HD * HD, 4 * seg * heads * HD),
    )(qkv, qkv)
    return memory, normer[:, 0]


def local_attention(qkv, start, heads):
    seg = qkv.shape[0]
    return pl.pallas_call(
        local_kernel,
        grid=(heads,),
        in_specs=[pl.BlockSpec(memory_space=pltpu.SMEM)]
        + [head_block(seg, heads, part) for part in range(3)],
        out_specs=pl.BlockSpec((seg, HD), lambda h: (0, h)),
        out_shape=jax.ShapeDtypeStruct((seg, heads * HD), f32),
        compiler_params=params(),
        cost_estimate=cost(40 * seg * seg * heads * HD, 10 * seg * heads * HD),
    )(start, qkv, qkv, qkv)


def recall(query, memory, normer):
    feature_q = feature(query.astype(f32))
    denominator = jnp.sum(feature_q * normer, axis=-1, keepdims=True) + 1.0
    inverse = 1.0 / denominator
    return feature_q, inverse, dot(feature_q, memory, 1, 0, highest) * inverse


def mix_kernel(gate_ref, query_ref, mix_ref, memory_ref, normer_ref, near_ref, far_ref, heads_ref, out_ref):
    heads = memory_ref.shape[0]
    half = near_ref.shape[1]
    for h in range(heads):
        columns = slice(h * HD, (h + 1) * HD)
        gate = gate_ref[h]
        _, _, recalled = recall(query_ref[:, columns], memory_ref[h], normer_ref[h : h + 1])
        mixture = gate * recalled + (1.0 - gate) * mix_ref[:, columns]
        heads_ref[:, columns] = mixture.astype(bf16)
    out_ref[:, :half] = dot(heads_ref[...], near_ref[...]).astype(bf16)
    out_ref[:, half:] = dot(heads_ref[...], far_ref[...]).astype(bf16)


def mix_and_project(gate, qkv, local_mix, memory, normer, weight):
    seg, inner = local_mix.shape
    width = 2 * weight[0].shape[1]
    return pl.pallas_call(
        mix_kernel,
        grid=(1,),
        in_specs=[
            pl.BlockSpec(memory_space=pltpu.SMEM),
            whole_block((seg, inner)),
            whole_block((seg, inner)),
            whole_block(memory.shape),
            whole_block(normer.shape),
            whole_block(weight[0].shape),
            whole_block(weight[1].shape),
        ],
        out_specs=[whole_block((seg, inner)), whole_block((seg, width))],
        out_shape=[
            jax.ShapeDtypeStruct((seg, inner), bf16),
            jax.ShapeDtypeStruct((seg, width), bf16),
        ],
        compiler_params=params(),
        cost_estimate=cost(2 * seg * inner * (width + 6 * HD), 8 * seg * inner + 2 * (seg + inner) * width),
    )(gate, qkv, local_mix, memory, normer, *weight)


def act_kernel(
    normed_ref, cot_ref, gate_near, gate_far, up_near, up_far, down_near, down_far,
    act_ref, gate_grad_ref, up_grad_ref,
):
    half = normed_ref.shape[1] // 2
    near, far = normed_ref[:, :half], normed_ref[:, half:]
    gated = dot(near, gate_near[...]) + dot(far, gate_far[...])
    upper = dot(near, up_near[...]) + dot(far, up_far[...])
    act_grad = dot(cot_ref[:, :half], down_near[...], 1, 1) + dot(cot_ref[:, half:], down_far[...], 1, 1)
    gate = jax.nn.sigmoid(gated)
    swish = gated * gate
    act_ref[...] = (swish * upper).astype(bf16)
    gate_grad_ref[...] = (act_grad * upper * (gate * (1.0 + gated * (1.0 - gate)))).astype(bf16)
    up_grad_ref[...] = (act_grad * swish).astype(bf16)


def activations(normed, cot, gate, up, down, tile):
    seg, width = normed.shape
    hidden = down[0].shape[0]
    half = width // 2
    into = pl.BlockSpec((half, tile), lambda j: (0, j))
    back = pl.BlockSpec((tile, half), lambda j: (j, 0))
    out = pl.BlockSpec((seg, tile), lambda j: (0, j))
    return pl.pallas_call(
        act_kernel,
        grid=(hidden // tile,),
        in_specs=[whole_block((seg, width))] * 2 + [into] * 4 + [back] * 2,
        out_specs=[out] * 3,
        out_shape=[jax.ShapeDtypeStruct((seg, hidden), bf16)] * 3,
        compiler_params=params(),
        cost_estimate=cost(6 * seg * width * hidden, 6 * hidden * width + 4 * seg * width + 6 * seg * hidden),
    )(normed, cot, *gate, *up, *down)


def width_kernel(weight_dim, count, *refs):
    lefts, weights, out_ref = refs[:count], refs[count:-1], refs[-1]
    half = out_ref.shape[1] // 2
    tile = weights[0].shape[1 - weight_dim]
    for place in range(2):
        total = dot(lefts[0][...], weights[place][...], 1, weight_dim)
        for k in range(1, count):
            total = total + dot(lefts[k][...], weights[2 * k + place][...], 1, weight_dim)
        start = pl.multiple_of(place * half + pl.program_id(0) * tile, tile)
        out_ref[:, pl.ds(start, tile)] = total.astype(bf16)


def into_width(lefts, weights, weight_dim, tile=256):
    seg, inner = lefts[0].shape
    half = weights[0][0].shape[1 - weight_dim]
    shape = (inner, tile) if weight_dim == 0 else (tile, inner)
    block = pl.BlockSpec(shape, lambda j: (0, j) if weight_dim == 0 else (j, 0))
    count = len(lefts)
    return pl.pallas_call(
        functools.partial(width_kernel, weight_dim, count),
        grid=(half // tile,),
        in_specs=[whole_block((seg, inner))] * count + [block] * (2 * count),
        out_specs=whole_block((seg, 2 * half)),
        out_shape=jax.ShapeDtypeStruct((seg, 2 * half), bf16),
        compiler_params=params(),
        cost_estimate=cost(
            4 * count * seg * inner * half, count * (2 * seg * inner + 4 * inner * half) + 4 * seg * half
        ),
    )(*lefts, *[half_weight for weight in weights for half_weight in weight])


def recall_grad_kernel(
    gate_ref, keep_ref, mid_ref, near_ref, far_ref, query_ref, mix_ref, memory_ref, normer_ref,
    local_ref, query_grad_ref, memory_grad_ref, normer_grad_ref, gate_grad_ref,
):
    h = pl.program_id(0)
    half = near_ref.shape[1]
    gate = gate_ref[h]
    keep = keep_ref[0]
    mixture_grad = dot(mid_ref[:, :half], near_ref[...], 1, 1) + dot(mid_ref[:, half:], far_ref[...], 1, 1)
    normer = normer_ref[0, :1]
    feature_q, inverse, recalled = recall(query_ref[...], memory_ref[0], normer)
    gate_grad_ref[0] = jnp.broadcast_to(
        jnp.sum(mixture_grad * (recalled - mix_ref[...]), axis=0, keepdims=True), gate_grad_ref.shape[1:]
    )
    local_ref[...] = ((1.0 - gate) * mixture_grad).astype(bf16)
    share = gate * mixture_grad * inverse
    weigh = jnp.sum(share * recalled, axis=-1, keepdims=True)
    memory_grad_ref[0] = dot(feature_q, share, 0, 0, highest) * keep
    normer_grad_ref[0] = jnp.broadcast_to(
        -jnp.sum(weigh * feature_q, axis=0, keepdims=True) * keep, normer_grad_ref.shape[1:]
    )
    query_grad_ref[...] = (dot(share, memory_ref[0], 1, 1, highest) - weigh * normer) * slope(
        query_ref[...].astype(f32)
    )


def recall_backward(gate, keep, mid_seg, weight, qkv, local_mix, memory, normer):
    seg, width = mid_seg.shape
    heads = memory.shape[0]
    half = width // 2
    columns = pl.BlockSpec((seg, HD), lambda h: (0, h))
    row_block = pl.BlockSpec((1, 8, HD), lambda h: (h, 0, 0))
    memory_block = pl.BlockSpec((1, HD, HD), lambda h: (h, 0, 0))
    normer_rows = jnp.broadcast_to(normer[:, None], (heads, 8, HD))
    local_grad, query_grad, memory_grad, normer_grad, gate_grad = pl.pallas_call(
        recall_grad_kernel,
        grid=(heads,),
        in_specs=[
            pl.BlockSpec(memory_space=pltpu.SMEM),
            pl.BlockSpec(memory_space=pltpu.SMEM),
            whole_block((seg, width)),
            pl.BlockSpec((HD, half), lambda h: (h, 0)),
            pl.BlockSpec((HD, half), lambda h: (h, 0)),
            columns,
            columns,
            memory_block,
            row_block,
        ],
        out_specs=[columns, columns, memory_block, row_block, row_block],
        out_shape=[
            jax.ShapeDtypeStruct((seg, heads * HD), bf16),
            jax.ShapeDtypeStruct((seg, heads * HD), f32),
            jax.ShapeDtypeStruct((heads, HD, HD), f32),
            jax.ShapeDtypeStruct((heads, 8, HD), f32),
            jax.ShapeDtypeStruct((heads, 8, HD), f32),
        ],
        compiler_params=params(),
        cost_estimate=cost(2 * seg * heads * HD * (width + 12 * HD), 2 * seg * width + 12 * seg * heads * HD),
    )(gate, keep, mid_seg, *weight, qkv, local_mix, memory, normer_rows)
    return local_grad, query_grad, memory_grad, normer_grad[:, 0], jnp.sum(gate_grad[:, 0], axis=-1)


def local_grad_kernel(
    start_ref, query_ref, key_ref, value_ref, local_ref, extra_ref, query_grad_ref, key_grad_ref, value_grad_ref
):
    scale = float(HD) ** (-0.5)
    query, key, local = query_ref[...], key_ref[...], local_ref[...]
    soft = soft_rows(query, key, start_ref[0])
    value_grad_ref[...] = dot(soft.astype(bf16), local, 0, 0)
    prob_grad = dot(local, value_ref[...], 1, 1)
    score_grad = (soft * (prob_grad - jnp.sum(soft * prob_grad, axis=-1, keepdims=True))).astype(bf16)
    query_grad_ref[...] = (dot(score_grad, key) * scale + extra_ref[...]).astype(bf16)
    key_grad_ref[...] = dot(score_grad, query, 0, 0) * scale


def local_backward(start, qkv, local_grad, query_extra, heads):
    seg = qkv.shape[0]
    columns = pl.BlockSpec((seg, HD), lambda h: (0, h))
    return pl.pallas_call(
        local_grad_kernel,
        grid=(heads,),
        in_specs=[pl.BlockSpec(memory_space=pltpu.SMEM)]
        + [head_block(seg, heads, part) for part in range(3)]
        + [columns, columns],
        out_specs=[columns, columns, columns],
        out_shape=[
            jax.ShapeDtypeStruct((seg, heads * HD), bf16),
            jax.ShapeDtypeStruct((seg, heads * HD), f32),
            jax.ShapeDtypeStruct((seg, heads * HD), f32),
        ],
        compiler_params=params(),
        cost_estimate=cost(80 * seg * seg * heads * HD, 20 * seg * heads * HD),
    )(start, qkv, qkv, qkv, local_grad, query_extra)


def back_kernel(
    rows_ref, qkv_ref, query_grad_ref, key_grad_ref, value_grad_ref, memory_ref, normer_ref,
    near_ref, far_ref, grads_ref, part_ref, gain_ref,
):
    heads = memory_ref.shape[0]
    inner = heads * HD
    half = near_ref.shape[0]
    grads_ref[:, :inner] = query_grad_ref[...]
    for h in range(heads):
        columns = slice(h * HD, (h + 1) * HD)
        key = qkv_ref[:, inner + h * HD : inner + (h + 1) * HD].astype(f32)
        value = qkv_ref[:, 2 * inner + h * HD : 2 * inner + (h + 1) * HD].astype(f32)
        key_extra = dot(value, memory_ref[h], 1, 1, highest) + normer_ref[h : h + 1]
        grads_ref[:, inner + h * HD : inner + (h + 1) * HD] = (
            key_grad_ref[:, columns] + key_extra * slope(key)
        ).astype(bf16)
        grads_ref[:, 2 * inner + h * HD : 2 * inner + (h + 1) * HD] = (
            value_grad_ref[:, columns] + dot(feature(key), memory_ref[h], 1, 0, highest)
        ).astype(bf16)
    rows = rows_ref[...].astype(f32)
    scale = lax.rsqrt(jnp.mean(rows * rows, axis=-1, keepdims=True) + epsilon)
    for place, weight_ref in enumerate((near_ref, far_ref)):
        columns = slice(place * half, (place + 1) * half)
        part = dot(grads_ref[...], weight_ref[...], 1, 1)
        part_ref[:, columns] = part.astype(bf16)
        gain_ref[:, columns] = jnp.broadcast_to(
            jnp.sum(part * (rows[:, columns] * scale), axis=0, keepdims=True), (8, half)
        )


def attention_back(rows, qkv, query_grad, key_grad, value_grad, memory, normer, weight):
    seg, width = rows.shape
    columns = qkv.shape[1]
    inner = columns // 3
    grads, part, gain = pl.pallas_call(
        back_kernel,
        grid=(1,),
        in_specs=[
            whole_block((seg, width)),
            whole_block((seg, columns)),
            whole_block((seg, inner)),
            whole_block((seg, inner)),
            whole_block((seg, inner)),
            whole_block(memory.shape),
            whole_block(normer.shape),
            whole_block((width // 2, columns)),
            whole_block((width // 2, columns)),
        ],
        out_specs=[whole_block((seg, columns)), whole_block((seg, width)), whole_block((8, width))],
        out_shape=[
            jax.ShapeDtypeStruct((seg, columns), bf16),
            jax.ShapeDtypeStruct((seg, width), bf16),
            jax.ShapeDtypeStruct((8, width), f32),
        ],
        compiler_params=params(),
        cost_estimate=cost(2 * seg * columns * (width + 4 * HD), 2 * (width * columns + 2 * seg * width + 3 * seg * columns)),
    )(rows, qkv, query_grad, key_grad, value_grad, memory, normer, *weight)
    return grads, part, gain[0]


def grad_kernel(count, has_more, *refs):
    lefts, rights = refs[:count], refs[count : 2 * count]
    total = dot(lefts[0][...], rights[0][...], 0, 0)
    for left, right in zip(lefts[1:], rights[1:]):
        total = total + dot(left[...], right[...], 0, 0)
    if has_more:
        total = total + refs[2 * count][...].astype(f32)
    refs[-1][...] = total.astype(refs[-1].dtype)


def grad_product(lefts, rights, left_part, right_part, more=None, tile_i=256, tile_j=2048):
    seg = lefts[0].shape[0]
    height = lefts[0].shape[1] // left_part[1]
    length = rights[0].shape[1] // right_part[1]
    tile_i, tile_j = min(tile_i, height), min(tile_j, length)
    base_i, base_j = left_part[0] * (height // tile_i), right_part[0] * (length // tile_j)
    out_block = pl.BlockSpec((tile_i, tile_j), lambda i, j: (i, j))
    return pl.pallas_call(
        functools.partial(grad_kernel, len(lefts), more is not None),
        grid=(height // tile_i, length // tile_j),
        in_specs=[pl.BlockSpec((seg, tile_i), lambda i, j: (0, base_i + i)) for _ in lefts]
        + [pl.BlockSpec((seg, tile_j), lambda i, j: (0, base_j + j)) for _ in rights]
        + ([] if more is None else [out_block]),
        out_specs=out_block,
        out_shape=jax.ShapeDtypeStruct((height, length), bf16),
        compiler_params=params(),
        cost_estimate=cost(
            2 * len(lefts) * seg * height * length,
            2 * len(lefts) * seg * (height + length) + 4 * height * length,
        ),
    )(*lefts, *rights, *([] if more is None else [more]))


def inverse_rms(values):
    return lax.rsqrt(jnp.mean(values * values, axis=-1, keepdims=True) + epsilon)


def norm_pull(values, scale, gain, grad):
    weighted = gain * grad
    return scale * (
        weighted - values * (scale * scale) * jnp.mean(weighted * values, axis=-1, keepdims=True)
    )


def weight_grad(order, left_sides, right_sides, axis):
    def product(place, more=None):
        part = (place, 2)
        return grad_product(
            [order.place(left_sides[0]), *left_sides[1:]],
            right_sides,
            part if axis == 0 else (0, 1),
            part if axis == 1 else (0, 1),
            more,
        )

    return Collect(order, product, axis)


def on_device(
    hidden_in,
    out_cotangent,
    piece_start,
    query_weight,
    key_weight,
    value_weight,
    output_weight,
    gate_weight,
    up_weight,
    down_weight,
    attn_gain,
    mlp_gain,
    memory_gate,
):
    dp_index = lax.axis_index("dp")
    dp_count = lax.axis_size("dp")
    tensor_count = lax.axis_size("tensor")
    heads_here = memory_gate.shape[0]
    width = hidden_in.shape[2]
    blocks = half_order(dp_count)
    tile = 512
    order = Order()

    inward_table, outward_table = tables(dp_index, blocks)
    gate_sig = jax.nn.sigmoid(memory_gate)
    keep = jnp.where(dp_index == 0, 0.0, 1.0).astype(f32)[None]
    gain_columns = jnp.pad(jnp.stack([attn_gain, mlp_gain], axis=1), ((0, 0), (0, HD - 2)))
    qkvg = jnp.concatenate([query_weight, key_weight, value_weight, gain_columns], axis=1)
    qkv_width = qkvg.shape[1] - HD
    one = SimpleNamespace()
    two = SimpleNamespace()

    one.rows, two.rows = move_columns([hidden_in[0], hidden_in[1]], inward_table)
    order.done(one.rows)
    rows_one = OffloadGather(order, one.rows)
    rows_two = OffloadGather(order, two.rows)
    qkvg_spread = Spread(order, qkvg, 0)
    one.cot, two.cot = move_columns(
        [order.place(out_cotangent[0]), out_cotangent[1]], inward_table
    )
    order.done(one.cot)
    qkvg_spread.second()
    output_spread = Spread(order, output_weight, 1)
    qkvg_spread.third()
    one.rows_seg = rows_one.finish()

    gains = jnp.concatenate(
        [half[:, qkv_width : qkv_width + 2] for half in qkvg_spread.whole], axis=0
    )
    gains = jnp.transpose(gains.astype(f32))
    gain_one, gain_two = gains[0], gains[1]

    def project(now):
        now.seg_in, now.qkv = norm_qkv(
            order.place(now.rows_seg), gain_one, qkvg_spread.whole, qkv_width
        )
        order.done(now.qkv)

    def remember(now):
        memory, normer = segment_memory(order.place(now.qkv), heads_here)
        order.done(memory)
        now.scan = Scan(order, memory, normer, False)

    def attend(now, b):
        now.mix = local_attention(order.place(now.qkv), piece_start[b], heads_here)
        order.done(now.mix)

    def mix(now):
        now.memory, now.normer = now.scan.finish()
        now.heads_out, part = mix_and_project(
            gate_sig, order.place(now.qkv), now.mix, now.memory, now.normer,
            output_spread.whole,
        )
        order.done(now.heads_out)
        now.scatter = OffloadScatter(order, part)

    def norm_middle(now):
        now.middle = now.rows.astype(f32) + now.scatter.finish()
        now.scale_two = inverse_rms(now.middle)
        normed = (now.middle * now.scale_two * gain_two).astype(bf16)
        now.gather = OffloadGather(order, order.done(normed))

    def activate(now):
        now.act, now.gate_grad, now.up_grad = activations(
            order.place(now.seg_two), now.cot_seg, gate_spread.whole, up_spread.whole,
            down_spread.whole, tile,
        )
        order.done(now.act)

    def feed_back(now):
        part = into_width(
            [order.place(now.gate_grad), now.up_grad], [gate_spread.whole, up_spread.whole], 1
        )
        now.scatter = OffloadScatter(order, order.done(part))

    def feed_rows(now):
        part = into_width([order.place(now.act)], [down_spread.whole], 0)
        now.feed_rows = OffloadScatter(order, order.done(part))

    def norm_out(now):
        rows = now.feed_rows.finish()
        now.hidden_out = order.done((now.middle + rows).astype(bf16))

    def norm_grad(now):
        grad = now.scatter.finish()
        middle, scale = now.middle, now.scale_two
        now.gain_two_term = jnp.sum(grad * middle * scale, axis=0)
        now.middle_grad = now.cot.astype(f32) + norm_pull(middle, scale, gain_two, grad)
        now.gather = OffloadGather(order, order.done(now.middle_grad.astype(bf16)))

    def recall_back(now):
        local_grad, query_extra, memory_grad, normer_grad, now.gate_term = recall_backward(
            gate_sig, keep, order.place(now.mid_seg), output_spread.whole, now.qkv,
            now.mix, now.memory, now.normer,
        )
        now.local = order.done(local_grad), query_extra
        now.scan = Scan(order, memory_grad, normer_grad, True)

    def local_back(now, b):
        now.grads = local_backward(
            piece_start[b], order.place(now.qkv), *now.local, heads_here
        )
        order.done(now.grads[0])

    def attention_backward(now):
        now.qkv_grad, part, now.gain_one_term = attention_back(
            order.place(now.rows_seg), now.qkv, *now.grads, *now.scan.finish(),
            qkvg_spread.whole,
        )
        order.done(now.qkv_grad)
        now.scatter = OffloadScatter(order, part)

    def norm_in_grad(now):
        own_rows = now.rows.astype(f32)
        now.hidden_grad = order.done(
            now.middle_grad
            + norm_pull(own_rows, inverse_rms(own_rows), gain_one, now.scatter.finish())
        )

    def small_messages():
        gate_sum = (one.gate_term + two.gate_term) * gate_sig * (1.0 - gate_sig)
        halves_here = len(blocks)
        half_width = width // halves_here
        by_half = [term.reshape(halves_here, half_width) for term in (one.gain_one_term + two.gain_one_term, one.gain_two_term + two.gain_two_term)]
        messages = []
        for offset in range(dp_count):
            pick = [blocks.index((offset, half)) for half in range(2)]
            message = jnp.concatenate(
                [term[k] for term in by_half for k in pick] + [jnp.pad(gate_sum, (0, HD - heads_here))]
            )
            messages.append(flip(message, offset) if offset else message)
        return messages

    project(one)
    output_spread.second()
    remember(one)
    attend(one, 0)
    one.scan.step()
    output_spread.third()
    one.scan.step()
    mix(one)
    gate_spread = Spread(order, gate_weight, 0)
    two.rows_seg = rows_two.finish()
    cot_one = Gather(order, one.cot)
    project(two)
    remember(two)
    attend(two, 1)
    two.scan.step()
    cot_one.second()
    two.scan.step()
    mix(two)
    cot_one.third()
    up_spread = Spread(order, up_weight, 0)
    norm_middle(one)
    cot_two = Gather(order, two.cot)
    gate_spread.second()
    one.cot_seg = cot_one.finish()
    up_spread.second()
    cot_two.second()
    gate_spread.third()
    down_spread = Spread(order, down_weight, 1)
    cot_two.third()
    norm_middle(two)
    up_spread.third()
    down_spread.second()
    two.cot_seg = cot_two.finish()
    down_spread.third()
    one.seg_two = one.gather.finish()

    activate(one)
    feed_back(one)
    two.seg_two = two.gather.finish()
    activate(two)
    feed_back(two)
    gate_collect = weight_grad(order, [one.seg_two, two.seg_two], [one.gate_grad, two.gate_grad], 0)
    norm_grad(one)
    up_collect = weight_grad(order, [one.seg_two, two.seg_two], [one.up_grad, two.up_grad], 0)
    down_collect = weight_grad(order, [one.act, two.act], [one.cot_seg, two.cot_seg], 1)
    norm_grad(two)
    gate_collect.second()
    up_collect.second()

    gate_collect.third()
    one.mid_seg = one.gather.finish()
    recall_back(one)
    local_back(one, 0)
    one.scan.step()
    one.scan.step()
    attention_backward(one)
    two.mid_seg = two.gather.finish()
    recall_back(two)
    local_back(two, 1)
    two.scan.step()
    two.scan.step()
    attention_backward(two)
    qkv_collect = weight_grad(order, [one.seg_in, two.seg_in], [one.qkv_grad, two.qkv_grad], 0)
    output_collect = weight_grad(order, [one.heads_out, two.heads_out], [one.mid_seg, two.mid_seg], 1)
    up_collect.third()
    qkv_collect.second()
    feed_rows(one)
    output_collect.second()
    gate_total = gate_collect.finish()
    down_collect.second()
    feed_rows(two)
    norm_in_grad(one)
    up_total = up_collect.finish()
    qkv_collect.third()
    output_collect.third()
    down_collect.third()
    messages = order.place(small_messages())
    norm_in_grad(two)
    output_grad = output_collect.finish()
    down_grad = down_collect.finish()
    norm_out(one)
    norm_out(two)
    qkv_total = qkv_collect.finish()
    block = width // dp_count
    small_sum = sum(order.place(messages))
    gain_part = small_sum[: 2 * block]
    gain_sum = gain_part
    for hop in range(1, tensor_count):
        gain_sum = gain_sum + send(
            gain_part, [(i, (i + hop) % tensor_count) for i in range(tensor_count)]
        )

    query_total, key_total, value_total = cut(qkv_total, 3, 1)
    return (
        move_columns([jnp.stack([one.hidden_out, two.hidden_out])], outward_table)[0],
        move_columns([jnp.stack([one.hidden_grad, two.hidden_grad])], outward_table)[0],
        query_total,
        key_total,
        value_total,
        output_grad,
        gate_total,
        up_total,
        down_grad,
        gain_sum[:block],
        gain_sum[block:],
        small_sum[2 * block : 2 * block + heads_here],
    )


def solution(mesh):
    rows = P(None, ("dp", "tensor"))
    inward = P("dp", "tensor")
    outward = P("tensor", "dp")
    return jax.shard_map(
        on_device,
        mesh=mesh,
        in_specs=(
            rows, rows, P(None, "dp"), inward, inward, inward, outward, inward, inward, outward,
            P("dp"), P("dp"), P("tensor"),
        ),
        out_specs=(
            rows, rows, inward, inward, inward, outward, inward, inward, outward,
            P("dp"), P("dp"), P("tensor"),
        ),
        check_vma=False,
    )
```
